256 devices in a mesh: ctx: 16 (over y_hi, x, core), smp: 16 (over y_lo, z).
Axes of the slice: x: 4, y: 4 (y_hi: 2, y_lo: 2; y = y_hi * 2 + y_lo), z: 8, core: 2. Of those that a mesh axis runs over, the one named last changes fastest.
Arguments:
- hidden_states: bfloat16 [64, 64, 5120], P('smp'), may hold values from -6 to 6
- query_weight: bfloat16 [5120, 5120], P('smp', 'ctx'), may hold values from -0.078125 to 0.078125
- kv_weight: bfloat16 [5120, 2048], P('smp', 'ctx'), may hold values from -0.078125 to 0.078125
- out_weight: bfloat16 [5120, 5120], P('smp', 'ctx'), may hold values from -0.078125 to 0.078125
- query_bias: bfloat16 [5120], P('ctx'), may hold values from -3 to 3
- kv_bias: bfloat16 [2048], P('ctx'), may hold values from -3 to 3
- prompt_kv: bfloat16 [4096, 2, 1024], P('ctx')
- parents: int32 [64, 64], P('smp'), may hold values from 0 to 62, as said below
- prefix_len: int32 [64], P('smp'), may hold values from 1024 to 4096, as said below
Outputs:
- layer_out: float32 [64, 64, 5120], P('smp', None, 'ctx')
The draws below stay inside these ranges and needn't reach their ends.
Inputs may be any that keep to these rules, and one draw needn't show every extreme that they name: parents[s, 0] = 0, and for n >= 1 the parent of node n is an earlier node. `prefix_len`: some sample sees the whole prompt.
All inputs are finite; a program needn't handle non-finite values.
Results may differ from the reference program's by a relative error of at most 0.009.
The reference program's roundings to bfloat16 on the way count: a program that leaves them out, or rounds other values in their place, can miss the bound.
Values may be sent and summed in bfloat16 or wider, within the bound.
A program may use at most 64 MiB of HBM per device.

```python
import jax
import jax.numpy as jnp
from jax import lax

D = 5120
HQ = 40
KVH = 8
HD = 128
NODES = 64
SAMPLES = 64
PROMPT = 4096


def draw_parents(key, part):
    node_ids = jnp.arange(NODES, dtype=jnp.int32)
    low_bound = jnp.broadcast_to(jnp.maximum(node_ids - 4, 0), (SAMPLES, NODES))
    high_bound = jnp.broadcast_to(jnp.maximum(node_ids, 1), (SAMPLES, NODES))
    drawn = jax.random.randint(key, (SAMPLES, NODES), low_bound, high_bound, dtype=jnp.int32)
    return drawn.at[0, NODES - 1].set(NODES - 2)


def draw_prefix_len(key, part):
    drawn = jax.random.randint(key, (SAMPLES,), PROMPT // 4, PROMPT + 1, dtype=jnp.int32)
    return drawn.at[0].set(PROMPT)


def draw_prompt_kv(key, part):
    full_shape = (PROMPT, 2, KVH * HD)
    base = jax.random.normal(key, full_shape, jnp.float32)
    key_rows = base[:, 0]
    return jnp.stack([key_rows, base[:, 1]], axis=1).astype(jnp.bfloat16)


def levels(key, extent, split, low, largest):
    factor_of = 1.0
    for axis_at, shards_of in split:
        heights = jax.random.uniform(jax.random.fold_in(jax.random.fold_in(key, 6), axis_at), (shards_of,), jnp.float32, low / len(split), largest / len(split))
        factor_of = factor_of * jnp.repeat(jnp.exp(heights), extent[axis_at] // shards_of).reshape((-1,) + (1,) * (len(extent) - 1 - axis_at))
    return factor_of


def normal_values(key, dims, width, most, pieces=(), kind=jnp.bfloat16):
    values = width * jax.random.normal(key, dims, jnp.float32)
    if pieces:
        values = values * levels(key, dims, pieces, -0.22, 0.18)
    return jnp.clip(values, -most, most).astype(kind)


def setup_inputs(seed: int = 0) -> dict:
    splits = jax.random.split(jax.random.key(seed), 10)
    hidden_states = normal_values(splits[0], (SAMPLES, NODES, D), 1.0, 6.0, ((0, 16),))
    query_weight = normal_values(splits[1], (D, HQ * HD), D ** -0.5, 0.078125, ((0, 16), (1, 16)))
    kv_weight = normal_values(splits[2], (D, 2 * KVH * HD), D ** -0.5, 0.078125, ((0, 16), (1, 16)))
    out_weight = normal_values(splits[3], (HQ * HD, D), (HQ * HD) ** -0.5, 0.078125, ((0, 16), (1, 16)))
    query_bias = normal_values(splits[4], (HQ * HD,), 0.5, 3.0, ((0, 16),))
    kv_bias = normal_values(splits[5], (2 * KVH * HD,), 0.5, 3.0, ((0, 16),))
    prompt_kv = draw_prompt_kv(jax.random.fold_in(splits[9], 71), 0)
    parents = draw_parents(jax.random.fold_in(splits[9], 71), 0)
    prefix_len = draw_prefix_len(jax.random.fold_in(splits[9], 71), 0)
    return {"hidden_states": hidden_states, "query_weight": query_weight, "kv_weight": kv_weight, "out_weight": out_weight, "query_bias": query_bias, "kv_bias": kv_bias, "prompt_kv": prompt_kv, "parents": parents, "prefix_len": prefix_len}


rope_theta = 1000000.0
neg_big = -1.0e30


def rounded(values):
    return lax.optimization_barrier(values.astype(jnp.bfloat16)).astype(jnp.float32)


def ancestors(parents):
    node_count = parents.shape[-1]
    node_ids = jnp.arange(node_count, dtype=jnp.int32)
    step_up = (parents[..., :, None] == node_ids[None, None, :]).astype(jnp.float32)
    step_up = step_up * (node_ids[:, None] > 0).astype(jnp.float32)[None]
    reach = step_up + jnp.eye(node_count, dtype=jnp.float32)[None]
    for squaring in range(max(node_count - 1, 1).bit_length()):
        reach = jnp.minimum(jnp.einsum("snm,smk->snk", reach, reach, precision=lax.Precision.HIGHEST), 1.0)
    return reach


def rotate(values, positions):
    midpoint = values.shape[-1] // 2
    frequency = rope_theta ** (-jnp.arange(midpoint, dtype=jnp.float32) / midpoint)
    angles = positions[:, None] * frequency[None, :]
    cosine = jnp.cos(angles)[:, None, :]
    sine_part = jnp.sin(angles)[:, None, :]
    lower_half = values[..., :midpoint]
    upper_half = values[..., midpoint:]
    return jnp.concatenate([lower_half * cosine - upper_half * sine_part, upper_half * cosine + lower_half * sine_part], axis=-1)


def reference(hidden_states, query_weight, kv_weight, out_weight, query_bias, kv_bias, prompt_kv, parents, prefix_len):
    total_rows = SAMPLES * NODES
    group = HQ // KVH
    flat = hidden_states.reshape(total_rows, D)
    query_lin = rounded(jnp.dot(flat, query_weight, preferred_element_type=jnp.float32) + query_bias.astype(jnp.float32))
    kv_lin = rounded(jnp.dot(flat, kv_weight, preferred_element_type=jnp.float32) + kv_bias.astype(jnp.float32))
    reach = ancestors(parents)
    positions = (prefix_len.astype(jnp.float32)[:, None] + jnp.sum(reach, axis=-1) - 1.0).reshape(total_rows)
    queries = rounded(rotate(query_lin.reshape(total_rows, HQ, HD), positions))
    tree_keys = rounded(rotate(kv_lin[:, :KVH * HD].reshape(total_rows, KVH, HD), positions))
    tree_values = kv_lin[:, KVH * HD:].reshape(total_rows, KVH, HD)
    prompt_keys = prompt_kv[:, 0].astype(jnp.float32).reshape(PROMPT, KVH, HD)
    prompt_values = prompt_kv[:, 1].astype(jnp.float32).reshape(PROMPT, KVH, HD)
    scale = HD ** -0.5
    prompt_ids = jnp.arange(PROMPT, dtype=jnp.int32)

    def one_sample(index):
        start = (index * NODES).astype(jnp.int32)
        query_rows = lax.dynamic_slice_in_dim(queries, start, NODES).reshape(NODES, KVH, group, HD)
        keys_here = lax.dynamic_slice_in_dim(tree_keys, start, NODES)
        values_here = lax.dynamic_slice_in_dim(tree_values, start, NODES)
        reach_here = lax.dynamic_index_in_dim(reach, index, 0, keepdims=False)
        limit = lax.dynamic_index_in_dim(prefix_len, index, 0, keepdims=False)
        prompt_mask = (prompt_ids < limit)[None, None, None, :]
        tree_mask = (reach_here > 0.5)[:, None, None, :]
        prompt_scores = jnp.einsum("nkgd,pkd->nkgp", query_rows, prompt_keys) * scale
        prompt_scores = jnp.where(prompt_mask, prompt_scores, neg_big)
        tree_scores = jnp.einsum("nkgd,mkd->nkgm", query_rows, keys_here) * scale
        tree_scores = jnp.where(tree_mask, tree_scores, neg_big)
        top = jnp.maximum(jnp.max(prompt_scores, axis=-1), jnp.max(tree_scores, axis=-1))
        prompt_weights = jnp.where(prompt_mask, jnp.exp(prompt_scores - top[..., None]), 0.0)
        tree_weights = jnp.where(tree_mask, jnp.exp(tree_scores - top[..., None]), 0.0)
        total = jnp.sum(prompt_weights, axis=-1) + jnp.sum(tree_weights, axis=-1)
        summed = jnp.einsum("nkgp,pkd->nkgd", rounded(prompt_weights), prompt_values)
        summed = summed + jnp.einsum("nkgm,mkd->nkgd", rounded(tree_weights), values_here)
        return (summed / total[..., None]).astype(jnp.bfloat16).reshape(NODES, HQ * HD)

    attn = lax.map(one_sample, jnp.arange(SAMPLES, dtype=jnp.int32)).reshape(total_rows, HQ * HD)
    return jnp.dot(attn, out_weight, preferred_element_type=jnp.float32).reshape(SAMPLES, NODES, D)
```

```python
import functools

import jax
import jax.numpy as jnp
from jax import lax
from jax.experimental import pallas as pl
from jax.experimental.pallas import tpu as pltpu
from jax.sharding import PartitionSpec as P

MESH = pl.DeviceIdType.MESH
HD = 128
ROWS = 256
BLOCK = 320
Z = 8
QKV_ROWS, QKV_FIRST = 1120, 480
OUT_ROWS, OUT_FIRST = 800, 352
KEYS = 1024
NEG = -1e30
ROPE_THETA = 1000000.0
LOG2E = 1.4426950408889634
COPIES = 160


def dot(a, b):
    return lax.dot_general(a, b, (((1,), (0,)), ((), ())), preferred_element_type=jnp.float32)


def dot_t(a, b):
    return lax.dot_general(a, b, (((1,), (1,)), ((), ())), preferred_element_type=jnp.float32)


def kernel(
    h_hbm, wq_ref, wkv_ref, wo_ref, qb_ref, kvb_ref, prompt_hbm, par_ref, freq_ref, plen_ref,
    out_ref,
    hv, wbuf, obuf, pbuf, abuf, qx, qr, tk, tv, tsend, qs, reach_own, cosb, sinb,
    ss, rs, ls,
):
    j = lax.axis_index("ctx")
    i = lax.axis_index("smp")
    core = j % 2
    x = (j // 2) % 4
    yh = j // 8
    yl = i // Z
    z = i % Z
    head = j // 2
    sib = j + 1 - 2 * core
    other_y = (1 - yl) * Z + z

    def zat(d):
        return (z + d + Z) % Z

    counter = [0]
    started = []

    def new():
        counter[0] += 1
        return counter[0] - 1

    def send(k, src, dst, ctx, smp):
        copy = pltpu.make_async_remote_copy(
            src_ref=src, dst_ref=dst, send_sem=ss.at[k], recv_sem=rs.at[k],
            device_id={"ctx": ctx, "smp": smp}, device_id_type=MESH,
        )
        copy.start()
        started.append(copy)

    def landed(k, region):
        pltpu.make_async_copy(region, region, rs.at[k]).wait()

    barrier = pltpu.get_barrier_semaphore()
    for step in range(1, 16):
        pl.semaphore_signal(barrier, inc=1, device_id={"ctx": (j + step) % 16, "smp": i}, device_id_type=MESH)
    for smp in (yl * Z + zat(1), yl * Z + zat(-1), other_y):
        pl.semaphore_signal(barrier, inc=1, device_id={"ctx": j, "smp": smp}, device_id_type=MESH)
    for at in range(4):
        pl.semaphore_signal(
            barrier, inc=1, device_id={"ctx": ((1 - yh) * 4 + at) * 2 + core, "smp": other_y}, device_id_type=MESH
        )
    hcopy = pltpu.make_async_copy(h_hbm, hv, ls.at[0])
    hcopy.start()

    wq = wq_ref[...]
    main = jnp.where(core == 1, wq[:, 64:320], wq[:, 0:256])
    tail = jnp.where(core == 1, wq[:, 0:64], wq[:, 256:320])
    wbuf[i, 0:320, :] = main[:, 0:128]
    wbuf[i, 320:640, :] = main[:, 128:256]
    wbuf[i, 640:960, :] = wkv_ref[...]
    wbuf[i, 960:1120, :] = jnp.concatenate([tail[0:160], tail[160:320]], axis=1)
    pl.semaphore_wait(barrier, 22)

    class Gather:
        def __init__(self, buf, rows, first):
            self.buf, self.rows, self.first, self.half = buf, rows, first, rows // 2
            self.up = [new() for _ in range(4)]
            self.down = [new() for _ in range(4)]
            self.up2 = [new() for _ in range(4)]
            self.down2 = [new() for _ in range(4)]
            self.ya = new()
            self.yb = [new() for _ in range(8)]

        def at(self, y, d, lo, hi):
            return self.buf.at[y * Z + zat(d), pl.ds(lo, hi - lo), :]

        def ship(self, k, y, d, lo, hi, smp):
            region = self.at(y, d, lo, hi)
            send(k, region, region, j, smp)

        def start(self):
            self.ship(self.up[0], yl, 0, 0, self.rows, yl * Z + zat(1))
            self.ship(self.down[0], yl, 0, 0, self.rows, yl * Z + zat(-1))
            self.ship(self.ya, yl, 0, 0, self.first, other_y)
            self.ship(self.yb[0], yl, 0, self.first, self.rows, other_y)

        def start2(self):
            landed(self.ya, self.at(1 - yl, 0, 0, self.first))
            self.ship(self.up2[0], 1 - yl, 0, 0, self.first, yl * Z + zat(1))
            self.ship(self.down2[0], 1 - yl, 0, 0, self.first, yl * Z + zat(-1))

        def ring(self, s):
            last = s == 3
            mid = self.half if last else self.rows
            low = self.half if last else 0
            landed(self.up[s - 1], self.at(yl, -s, 0, self.rows))
            self.ship(self.up[s], yl, -s, 0, mid, yl * Z + zat(1))
            self.ship(self.yb[2 * s - 1], yl, -s, self.first, self.rows, other_y)
            landed(self.down[s - 1], self.at(yl, s, 0, self.rows))
            self.ship(self.down[s], yl, s, low, self.rows, yl * Z + zat(-1))
            self.ship(self.yb[2 * s], yl, s, self.first, self.rows, other_y)

        def ring2(self, s):
            last = s == 3
            mid = self.first // 2 if last else self.first
            low = self.first // 2 if last else 0
            landed(self.up2[s - 1], self.at(1 - yl, -s, 0, self.first))
            self.ship(self.up2[s], 1 - yl, -s, 0, mid, yl * Z + zat(1))
            landed(self.down2[s - 1], self.at(1 - yl, s, 0, self.first))
            self.ship(self.down2[s], 1 - yl, s, low, self.first, yl * Z + zat(-1))

        def far(self):
            landed(self.up[3], self.at(yl, 4, 0, self.half))
            landed(self.down[3], self.at(yl, 4, self.half, self.rows))
            self.ship(self.yb[7], yl, 4, self.first, self.rows, other_y)

        def finish(self):
            landed(self.up2[3], self.at(1 - yl, 4, 0, self.first // 2))
            landed(self.down2[3], self.at(1 - yl, 4, self.first // 2, self.first))
            for k, d in zip(self.yb, (0, -1, 1, -2, 2, -3, 3, 4)):
                landed(k, self.at(1 - yl, d, self.first, self.rows))

    gqkv = Gather(wbuf, QKV_ROWS, QKV_FIRST)
    gout = Gather(obuf, OUT_ROWS, OUT_FIRST)
    gqkv.start()

    own = pltpu.make_async_copy(prompt_hbm.at[head], pbuf.at[j], ls.at[1])
    own.start()
    row_k = [new() for _ in range(3)]
    cross_k = [new() for _ in range(4)]
    sib_k = [new() for _ in range(8)]
    for step in range(1, 4):
        to = yh * 4 + (x + step) % 4
        send(row_k[step - 1], prompt_hbm.at[to], pbuf.at[j], to * 2 + core, i)
    for step in range(4):
        to = (1 - yh) * 4 + (x + step) % 4
        send(cross_k[step], prompt_hbm.at[to], pbuf.at[j], to * 2 + core, other_y)
    send(sib_k[0], prompt_hbm.at[head], pbuf.at[j], sib, i)

    wo = wo_ref[...]
    obuf[i, 0:320, :] = wo[:, 0:128]
    obuf[i, 320:640, :] = wo[:, 128:256]
    obuf[i, 640:800, :] = jnp.concatenate([wo[0:160, 256:320], wo[160:320, 256:320]], axis=1)

    m_id = lax.broadcasted_iota(jnp.int32, (ROWS, ROWS), 0)
    n_id = lax.broadcasted_iota(jnp.int32, (ROWS, ROWS), 1)
    parent = par_ref[...] + (lax.broadcasted_iota(jnp.int32, (1, ROWS), 1) // 64) * 64
    hit = ((m_id == parent) & (n_id % 64 > 0)) | (m_id == n_id)
    reached = jnp.where(hit, 1.0, 0.0).astype(jnp.bfloat16)
    for _ in range(6):
        reached = jnp.minimum(dot(reached, reached), 1.0).astype(jnp.bfloat16)
    identity = jnp.where(m_id == n_id, 1.0, 0.0).astype(jnp.bfloat16)
    reach = dot_t(identity, reached)
    reach_own[...] = jnp.where(core == 0, reach[0:128, 0:128], reach[128:256, 128:256])
    row_id = lax.broadcasted_iota(jnp.int32, (ROWS, 1), 0)
    prefix = jnp.where(
        row_id < 128,
        jnp.where(row_id < 64, plen_ref[0], plen_ref[1]),
        jnp.where(row_id < 192, plen_ref[2], plen_ref[3]),
    ).astype(jnp.float32)
    positions = prefix + jnp.sum(reach, axis=1, keepdims=True) - 1.0
    angles = positions * freq_ref[...]
    lane = lax.broadcasted_iota(jnp.int32, (1, HD), 1)
    cosb[...] = jnp.cos(angles)
    sinb[...] = jnp.sin(angles) * jnp.where(lane < 64, -1.0, 1.0)

    def rope(v, cosine, sine):
        turned = jnp.concatenate([v[:, 64:128], v[:, 0:64]], axis=1)
        return v * cosine + turned * sine

    gqkv.start2()
    gqkv.ring(1)
    for step in range(1, 4):
        src = (yh * 4 + (x - step + 4) % 4) * 2 + core
        landed(row_k[step - 1], pbuf.at[src])
        send(sib_k[step], pbuf.at[src], pbuf.at[src], sib, i)
    gqkv.ring2(1)
    gqkv.ring(2)
    for step in range(4):
        src = ((1 - yh) * 4 + (x - step + 4) % 4) * 2 + core
        landed(cross_k[step], pbuf.at[src])
        send(sib_k[4 + step], pbuf.at[src], pbuf.at[src], sib, i)
    gqkv.ring2(2)
    gqkv.ring(3)
    gqkv.ring2(3)
    gqkv.far()
    gout.start()
    hcopy.wait()
    gqkv.finish()

    acc_q = jnp.zeros((ROWS, 256), jnp.float32)
    acc_r = jnp.zeros((ROWS, 192), jnp.float32)

    def project(p, carry):
        acc_q, acc_r = carry
        hk = hv[:, pl.ds(pl.multiple_of(p * 640, 128), 640)]
        wa, wb = wbuf.at[2 * p], wbuf.at[2 * p + 1]
        w_main = jnp.concatenate(
            [
                jnp.concatenate([wa[0:320, :], wa[320:640, :]], axis=1),
                jnp.concatenate([wb[0:320, :], wb[320:640, :]], axis=1),
            ],
            axis=0,
        )
        ta, tb = wa[960:1120, :], wb[960:1120, :]
        w_tail = jnp.concatenate([ta[:, 0:64], ta[:, 64:128], tb[:, 0:64], tb[:, 64:128]], axis=0)
        w_kv = jnp.concatenate([wa[640:960, :], wb[640:960, :]], axis=0)
        w_rest = jnp.concatenate([w_kv, w_tail], axis=1)
        return acc_q + dot(hk, w_main), acc_r + dot(hk, w_rest)

    acc_q, acc_r = lax.fori_loop(0, 8, project, (acc_q, acc_r))
    qb = qb_ref[...].astype(jnp.float32)
    qb_main = jnp.where(core == 1, qb[:, 64:320], qb[:, 0:256])
    qb_tail = jnp.where(core == 1, qb[:, 0:64], qb[:, 256:320])

    kv = (acc_r[:, 0:128] + kvb_ref[...].astype(jnp.float32)).astype(jnp.bfloat16)
    kvf = kv.astype(jnp.float32)
    tsend[...] = jnp.where(j < 8, rope(kvf, cosb[...], sinb[...]), kvf).astype(jnp.bfloat16)
    tree_k = [[new(), new()], [new(), new()]]
    for part, buf in ((0, tk), (1, tv)):
        for to_core in range(2):
            k = tree_k[part][to_core]
            to = (j % 8) * 2 + to_core
            src = tsend.at[pl.ds(to_core * 128, 128), :]

            @pl.when((j // 8 == part) & (to == j))
            def _():
                pltpu.make_async_copy(src, buf, rs.at[k]).start()

            @pl.when((j // 8 == part) & (to != j))
            def _():
                pltpu.make_async_remote_copy(
                    src_ref=src, dst_ref=buf, send_sem=ss.at[k], recv_sem=rs.at[k],
                    device_id={"ctx": to, "smp": i}, device_id_type=MESH,
                ).start()

    qx[:, 0:256] = (acc_q + qb_main).astype(jnp.bfloat16)
    qx[:, 256:384] = jnp.concatenate(
        [(acc_r[:, 128:192] + qb_tail).astype(jnp.bfloat16), jnp.zeros((ROWS, 64), jnp.bfloat16)], axis=1
    )
    qk = new()
    other_rows = pl.ds(pl.multiple_of((1 - core) * 128, 128), 128)
    own_rows = pl.ds(pl.multiple_of(core * 128, 128), 128)
    send(qk, qx.at[other_rows, :], qr, sib, i)
    gout.start2()
    gout.ring(1)
    landed(qk, qr)
    mine = qx[own_rows, :]
    theirs = qr[...]
    qa = jnp.where(core == 0, mine, theirs).astype(jnp.float32)
    qc = jnp.where(core == 0, theirs, mine).astype(jnp.float32)
    cosine, sine = cosb[own_rows, :], sinb[own_rows, :]
    heads = [
        qa[:, 0:128],
        qa[:, 128:256],
        jnp.concatenate([qa[:, 256:320], qc[:, 256:320]], axis=1),
        qc[:, 0:128],
        qc[:, 128:256],
    ]
    for g in range(5):
        rotated = rope(heads[g], cosine, sine).astype(jnp.bfloat16)
        for s in range(2):
            qs[s, g * 64 : (g + 1) * 64, :] = rotated[s * 64 : (s + 1) * 64, :]
    for to_core in range(2):

        @pl.when(core == to_core)
        def _():
            landed(tree_k[0][to_core], tk)
            landed(tree_k[1][to_core], tv)

    own.wait()
    for step in range(8):
        if step < 4:
            src = (yh * 4 + (x - step + 4) % 4) * 2 + 1 - core
        else:
            src = ((1 - yh) * 4 + (x - (step - 4) + 4) % 4) * 2 + 1 - core
        landed(sib_k[step], pbuf.at[src])

    factor = HD ** (-0.5) * LOG2E

    def attend(s):
        q = qs[s]
        allowed = jnp.concatenate([reach_own[s * 64 : (s + 1) * 64, :]] * 5, axis=0) > 0.5
        scores = jnp.where(allowed, dot_t(q, tk[...]) * factor, NEG)
        top = jnp.max(scores, axis=1, keepdims=True)
        weights = jnp.exp2(scores - top)
        total = jnp.sum(weights, axis=1, keepdims=True)
        acc = dot(weights.astype(jnp.bfloat16), tv[...])
        limit = jnp.where(core == 0, plen_ref[s], plen_ref[2 + s])

        def step(n, carry):
            top, total, acc = carry
            keys = pbuf[pl.ds(4 * n, 4), 0:256, :].reshape(KEYS, HD)
            values = pbuf[pl.ds(4 * n, 4), 256:512, :].reshape(KEYS, HD)
            at = lax.broadcasted_iota(jnp.int32, (1, KEYS), 1) + n * KEYS
            scores = jnp.where(at < limit, dot_t(q, keys) * factor, NEG)
            new_top = jnp.maximum(top, jnp.max(scores, axis=1, keepdims=True))
            weights = jnp.exp2(scores - new_top)
            shrink = jnp.exp2(top - new_top)
            total = total * shrink + jnp.sum(weights, axis=1, keepdims=True)
            acc = acc * shrink + dot(weights.astype(jnp.bfloat16), values)
            return new_top, total, acc

        top, total, acc = lax.fori_loop(0, 4, step, (top, total, acc))
        return (acc / total).astype(jnp.bfloat16)

    ab = [[new() for _ in range(15)] for _ in range(2)]
    opp = (1 - yh) * 4 + x

    def piece(h, c, s):
        return abuf.at[h, pl.ds(pl.multiple_of(c * 128 + s * 64, 64), 64), :]

    def spread(ks, region, s):
        for step in range(1, 4):
            send(ks[step - 1], region, region, (yh * 4 + (x + step) % 4) * 2 + core, i)
        send(ks[3], region, region, sib, i)

    for s in range(2):
        result = attend(s)
        for g in range(5):
            abuf[head, pl.ds(pl.multiple_of(core * 128 + s * 64, 64), 64), g * 128 : (g + 1) * 128] = result[
                g * 64 : (g + 1) * 64, :
            ]
        mine = piece(head, core, s)
        send(ab[s][14], mine, mine, opp * 2 + core, i)
        spread(ab[s][0:4], mine, s)
        gout.ring2(1 + s)
        gout.ring(2 + s)
    gout.ring2(3)
    gout.far()
    for s in range(2):
        theirs = piece(opp, core, s)
        landed(ab[s][14], theirs)
        spread(ab[s][4:8], theirs, s)
    for s in range(2):
        for row in range(2):
            for step in range(1, 4):
                at = (yh if row == 0 else 1 - yh) * 4 + (x - step + 4) % 4
                region = piece(at, core, s)
                landed(ab[s][4 * row + step - 1], region)
                send(ab[s][8 + 3 * row + step - 1], region, region, sib, i)
    gout.finish()
    for s in range(2):
        landed(ab[s][3], piece(head, 1 - core, s))
        landed(ab[s][7], piece(opp, 1 - core, s))
        for row in range(2):
            for step in range(1, 4):
                at = (yh if row == 0 else 1 - yh) * 4 + (x - step + 4) % 4
                landed(ab[s][8 + 3 * row + step - 1], piece(at, 1 - core, s))

    def combine(p, carry):
        acc_m, acc_t = carry
        wa, wb = obuf.at[2 * p], obuf.at[2 * p + 1]
        w_main = jnp.concatenate(
            [
                jnp.concatenate([wa[0:320, :], wa[320:640, :]], axis=1),
                jnp.concatenate([wb[0:320, :], wb[320:640, :]], axis=1),
            ],
            axis=0,
        )
        ta, tb = wa[640:800, :], wb[640:800, :]
        w_tail = jnp.concatenate([ta[:, 0:64], ta[:, 64:128], tb[:, 0:64], tb[:, 64:128]], axis=0)
        a = abuf[p]
        return acc_m + dot(a, w_main), acc_t + dot(a, w_tail)

    acc_m, acc_t = lax.fori_loop(
        0, 8, combine, (jnp.zeros((ROWS, 256), jnp.float32), jnp.zeros((ROWS, 64), jnp.float32))
    )
    out_ref[:, 0:256] = acc_m
    out_ref[:, 256:320] = acc_t

    for copy in started:
        copy.wait_send()
    for part in range(2):
        for to_core in range(2):
            k = tree_k[part][to_core]
            to = (j % 8) * 2 + to_core

            @pl.when((j // 8 == part) & (to != j))
            def _():
                src = tsend.at[pl.ds(to_core * 128, 128), :]
                pltpu.make_async_copy(src, src, ss.at[k]).wait()

    assert counter[0] <= COPIES, counter[0]


def shards(
    hidden_states, query_weight, kv_weight, out_weight, query_bias, kv_bias, prompt_kv, parents, prefix_len
):
    prompt = prompt_kv.reshape(256, 2, 8, HD).transpose(2, 1, 0, 3).reshape(8, 512, HD)
    frequency = ROPE_THETA ** (-jnp.arange(64, dtype=jnp.float32) / 64)
    frequency = jnp.tile(frequency, 2).reshape(1, HD)
    vmem = pl.BlockSpec(memory_space=pltpu.VMEM)
    anywhere = pl.BlockSpec(memory_space=pl.ANY)
    b16 = jnp.bfloat16
    out = pl.pallas_call(
        kernel,
        out_shape=jax.ShapeDtypeStruct((ROWS, BLOCK), jnp.float32),
        in_specs=[anywhere, vmem, vmem, vmem, vmem, vmem, anywhere, vmem, vmem, pl.BlockSpec(memory_space=pltpu.SMEM)],
        out_specs=vmem,
        scratch_shapes=[
            pltpu.VMEM((ROWS, 5120), b16),
            pltpu.VMEM((16, QKV_ROWS, 128), b16),
            pltpu.VMEM((16, OUT_ROWS, 128), b16),
            pltpu.VMEM((16, 512, 128), b16),
            pltpu.VMEM((8, ROWS, 640), b16),
            pltpu.VMEM((ROWS, 384), b16),
            pltpu.VMEM((128, 384), b16),
            pltpu.VMEM((128, 128), b16),
            pltpu.VMEM((128, 128), b16),
            pltpu.VMEM((ROWS, 128), b16),
            pltpu.VMEM((2, 320, 128), b16),
            pltpu.VMEM((128, 128), jnp.float32),
            pltpu.VMEM((ROWS, 128), jnp.float32),
            pltpu.VMEM((ROWS, 128), jnp.float32),
            pltpu.SemaphoreType.DMA((COPIES,)),
            pltpu.SemaphoreType.DMA((COPIES,)),
            pltpu.SemaphoreType.DMA((2,)),
        ],
        compiler_params=pltpu.CompilerParams(
            collective_id=0, has_side_effects=True, vmem_limit_bytes=56 * 1024 * 1024
        ),
    )(
        hidden_states.reshape(ROWS, 5120), query_weight, kv_weight, out_weight, query_bias.reshape(1, BLOCK),
        kv_bias.reshape(1, HD), prompt, parents.reshape(1, ROWS), frequency, prefix_len,
    )
    return out.reshape(4, 64, BLOCK)


def solution(mesh):
    return jax.shard_map(
        shards,
        mesh=mesh,
        in_specs=(
            P("smp", None, None),
            P("smp", "ctx"),
            P("smp", "ctx"),
            P("smp", "ctx"),
            P("ctx"),
            P("ctx"),
            P("ctx", None, None),
            P("smp", None),
            P("smp"),
        ),
        out_specs=P("smp", None, "ctx"),
        check_vma=False,
    )
```
